32 devices in a mesh: seq: 16 (over z, x, core), head: 2 (over y).
Axes of the slice: x: 2, y: 2, z: 4, core: 2. Of those that a mesh axis runs over, the one named last changes fastest.
Arguments:
- tokens: bfloat16 [2048, 2048], P('seq'), may hold values from -17 to 17, as said below
- q_weight: bfloat16 [2048, 2048], P(None, 'head'), may hold values from -0.125 to 0.125
- k_weight: bfloat16 [2048, 256], P(None, 'head'), may hold values from -0.3125 to 0.3125
- v_weight: bfloat16 [2048, 256], P(None, 'head'), may hold values from -0.125 to 0.125
- out_weight: bfloat16 [2048, 2048], P('head'), may hold values from -1.25 to 1.25
- summary: bfloat16 [1024, 16, 2, 256], P('seq', None, None, 'head'), may hold values from -12 to 12
- links: int32 [16], P('seq'), may hold values from -1 to 1023, as said below
Outputs:
- mixed: bfloat16 [2048, 2048], P('seq', 'head')
The draws below stay inside these ranges and needn't reach their ends.
Inputs may be any that keep to these rules, and one draw needn't show every extreme that they name: `tokens`: in the hidden draw rows have scales of their own. `links`: padding (-1) fills the tail of the list, and at least the first half of the slots are valid. Counting the valid slots by owner (id // 64), one owner has exactly 3 and none more.
All inputs are finite; a program needn't handle non-finite values.
Results may differ from the reference program's by a relative error of at most 0.01.
The reference program's roundings to bfloat16 on the way (of `queries` and `attended`) count: a program that leaves them out, or rounds other values in their place, can miss the bound.
Values may be sent and summed in bfloat16 or wider, within the bound.
A program may use at most 64 MiB of HBM per device.

```python
import math
import jax
import jax.numpy as jnp
from jax import lax

D = 2048
HEADS = 16
KV_HEADS = 2
HEAD_DIM = 128
SUM_ROWS = 16
LINK_DEV = 1
ENT_DEV = 64
MOST = 3
TOKENS = 2048
LINKS = 16
ENTITIES = 1024
N_SEQ = 16


def draw_tokens(key, part):
    key = jax.random.fold_in(key, 11)
    base = jax.random.normal(key, (TOKENS, D), jnp.float32)
    return jnp.clip(base, -6.0, 6.0).astype(jnp.bfloat16)


def draw_links(key, part):
    key = jax.random.fold_in(key, 23)
    keys_list = jax.random.split(key, 6)
    half = LINKS // 2
    valid_count = jax.random.randint(keys_list[0], (), half, LINKS)
    first_ranks = jax.random.permutation(keys_list[1], half)
    positions = jnp.arange(LINKS, dtype=jnp.int32)
    ranks = jnp.concatenate([first_ranks.astype(jnp.int32), positions[half:]])
    hot_owner = jax.random.randint(keys_list[2], (), 0, N_SEQ - 1)
    second_owner = (hot_owner + 1 + jax.random.randint(keys_list[3], (), 0, N_SEQ - 2)) % (N_SEQ - 1)
    lower = jnp.minimum(hot_owner, second_owner)
    upper = jnp.maximum(hot_owner, second_owner)
    offset = jax.random.randint(keys_list[5], (), 0, N_SEQ - 2)
    rest_rank = ranks - 5 * LINK_DEV
    cycled = (rest_rank + offset) % (N_SEQ - 2)
    cycled = cycled + (cycled >= lower).astype(jnp.int32)
    cycled = cycled + (cycled >= upper).astype(jnp.int32)
    owners = jnp.where(ranks < MOST, hot_owner, jnp.where(ranks < 5 * LINK_DEV, second_owner, cycled))
    local_ids = jax.random.randint(keys_list[4], (LINKS,), 0, ENT_DEV)
    entity_ids = owners * ENT_DEV + local_ids
    entity_ids = jnp.where(ranks == 5 * LINK_DEV, ENTITIES - 1, entity_ids)
    entity_ids = jnp.where(positions < valid_count, entity_ids, -1)
    return entity_ids.astype(jnp.int32)


def spiked(result, stream_key, source, target, parts, factor):
    def block_of(axis_at):
        return (jnp.arange(result.shape[axis_at]) // (result.shape[axis_at] // parts)).reshape((-1,) + (1,) * (result.ndim - 1 - axis_at))

    one_side = jax.random.permutation(stream_key, parts)[block_of(target)]
    far = (block_of(target) + parts // 2) % parts
    return jnp.where((block_of(source) == one_side) | (block_of(source) == far), factor * result, result)


def block_levels(rng, shape, cuts, low, top_value):
    level, own = 1.0, jax.random.fold_in(rng, 6)
    for dim, parts in cuts:
        heights = jnp.exp(jax.random.uniform(jax.random.fold_in(own, dim), (parts,), jnp.float32, low / len(cuts), top_value / len(cuts)))
        level = level * jnp.repeat(heights, shape[dim] // parts).reshape([-1 if axis == dim else 1 for axis in range(len(shape))])
    return level


def noise(rng, shape, width, reach, shards=(), kind=jnp.bfloat16):
    entries = width * jax.random.normal(rng, shape, jnp.float32)
    if shards:
        entries = entries * block_levels(rng, shape, shards, -0.22, 0.18)
    return jnp.clip(entries, -reach, reach).astype(kind)


def noise_with(rng, shape, spread, most, pieces, heavy, kind=jnp.bfloat16):
    result = spread * jax.random.normal(rng, shape, jnp.float32)
    if pieces:
        result = result * block_levels(rng, shape, pieces, -0.22, 0.18)
    return jnp.clip(spiked(result, jax.random.fold_in(rng, 3), *heavy), -most, most).astype(kind)


def setup_inputs(seed: int = 0) -> dict:
    key_of = jax.random.split(jax.random.key(seed), 8)
    return {
        "tokens": draw_tokens(jax.random.fold_in(key_of[7], 71), 0),
        "q_weight": noise(key_of[1], (D, HEADS * HEAD_DIM), D ** -0.5, 0.125, ((1, 2),)),
        "k_weight": noise(key_of[2], (D, KV_HEADS * HEAD_DIM), (D // 6) ** -0.5, 0.3125, ((1, 2),)),
        "v_weight": noise(key_of[3], (D, KV_HEADS * HEAD_DIM), D ** -0.5, 0.125, ((1, 2),)),
        "out_weight": noise_with(key_of[4], (HEADS * HEAD_DIM, D), (HEADS * HEAD_DIM // 40) ** -0.5, 1.25, ((0, 2),), (0, 1, 2, 2.0)),
        "summary": noise(key_of[5], (ENTITIES, SUM_ROWS, 2, KV_HEADS * HEAD_DIM), 2.0, 12.0, ((0, 16), (3, 2))),
        "links": draw_links(jax.random.fold_in(key_of[7], 71), 0),
    }


def reference(tokens, q_weight, k_weight, v_weight, out_weight, summary, links):
    highest = lax.Precision.HIGHEST
    tokens_wide = tokens.astype(jnp.float32)

    def project(matrix):
        return jnp.dot(tokens_wide, matrix.astype(jnp.float32), precision=highest).astype(jnp.bfloat16)
    queries = project(q_weight)
    keys = project(k_weight)
    values = project(v_weight)
    valid = links >= 0
    safe_ids = jnp.where(valid, links, 0).astype(jnp.int32)
    fetched = summary[safe_ids]
    link_keys = fetched[:, :, 0].reshape(LINKS * SUM_ROWS, KV_HEADS * HEAD_DIM)
    link_values = fetched[:, :, 1].reshape(LINKS * SUM_ROWS, KV_HEADS * HEAD_DIM)
    all_keys = jnp.concatenate([keys, link_keys], axis=0)
    all_values = jnp.concatenate([values, link_values], axis=0)
    allowed = jnp.concatenate([jnp.ones((TOKENS,), bool), jnp.repeat(valid, SUM_ROWS)])
    block_rows = math.gcd(TOKENS, 1024)
    per_group = HEADS // KV_HEADS
    scale_factor = 1.0 / math.sqrt(HEAD_DIM)
    outputs = []
    for head in range(HEADS):
        group = head // per_group
        key_head = all_keys[:, group * HEAD_DIM:(group + 1) * HEAD_DIM].astype(jnp.float32)
        value_head = all_values[:, group * HEAD_DIM:(group + 1) * HEAD_DIM].astype(jnp.float32)
        query_head = queries[:, head * HEAD_DIM:(head + 1) * HEAD_DIM].astype(jnp.float32)
        query_head = query_head.reshape(TOKENS // block_rows, block_rows, HEAD_DIM)

        def one_block(query_block):
            scores = jnp.dot(query_block, key_head.T, precision=highest) * scale_factor
            scores = jnp.where(allowed[None, :], scores, -1e+30)
            weights = jnp.exp(scores - lax.optimization_barrier(jnp.max(scores, axis=1, keepdims=True)))
            totals = lax.optimization_barrier(jnp.sum(weights, axis=1, keepdims=True))
            rounded = lax.optimization_barrier(weights.astype(jnp.bfloat16)).astype(jnp.float32)
            return jnp.dot(rounded, value_head, precision=highest) / totals
        outputs.append(lax.map(one_block, query_head).reshape(TOKENS, HEAD_DIM))
    attended = jnp.concatenate(outputs, axis=1).astype(jnp.bfloat16)
    mixed = jnp.dot(attended.astype(jnp.float32), out_weight.astype(jnp.float32), precision=highest)
    return mixed.astype(jnp.bfloat16)
```

```python
import functools
import math

import jax
import jax.numpy as jnp
from jax import lax
from jax.experimental import pallas as pl
from jax.experimental.pallas import tpu as pltpu
from jax.sharding import PartitionSpec as P

HEAD_DIM = 128
SUM_ROWS = 16
MOST = 3
MESH = pl.DeviceIdType.MESH
F32 = jnp.float32
BF16 = jnp.bfloat16


def each(low, high, step):
    if high - low <= 8:
        for i in range(low, high):
            step(i)
    else:
        lax.fori_loop(low, high, lambda i, carry: (step(i), carry)[1], 0)


def kernel(
    n, entities, link_dev,
    tok_hbm, qw_hbm, kw_hbm, vw_hbm, ow_hbm, sum_hbm, links_ref,
    out_ref,
    tok, qw, kvw, ow, summ, q, kv, rows, link_v, link_s, att, part, y_send, y_recv,
    load_sem, kv_recv, row_recv, link_recv, link_send,
    kv_send_a, kv_send_b, kv_send_c, row_send_a, row_send_b, row_send_c,
    y_send_sem, y_recv_sem,
):
    me = lax.axis_index("seq")
    hd = lax.axis_index("head")
    size = n // 4
    a, b, c = me // 4, (me // 2) % 2, me % 2
    slots = n * link_dev
    t = tok.shape[0]
    heads = q.shape[0] // t

    def ident(a_, b_, c_):
        return (a_ * 2 + b_) * 2 + c_

    loads = [
        pltpu.make_async_copy(tok_hbm, tok, load_sem.at[0]),
        pltpu.make_async_copy(kw_hbm, kvw.at[:, pl.ds(0, HEAD_DIM)], load_sem.at[1]),
        pltpu.make_async_copy(vw_hbm, kvw.at[:, pl.ds(HEAD_DIM, HEAD_DIM)], load_sem.at[2]),
        pltpu.make_async_copy(sum_hbm, summ, load_sem.at[3]),
        pltpu.make_async_copy(qw_hbm, qw, load_sem.at[4]),
        pltpu.make_async_copy(ow_hbm, ow, load_sem.at[5]),
    ]
    for item in loads:
        item.start()

    barrier = pltpu.get_barrier_semaphore()

    def greet(k):
        pl.semaphore_signal(
            barrier, inc=1, device_id=(lax.rem(me + k, n), hd), device_id_type=MESH
        )

    each(1, n, greet)
    pl.semaphore_signal(barrier, inc=1, device_id=(me, 1 - hd), device_id_type=MESH)

    lane = lax.broadcasted_iota(jnp.int32, (1, 128), 1)
    mine = jnp.full((1, 128), -1, jnp.int32)
    for i in range(link_dev):
        mine = jnp.where(lane == i, links_ref[i], mine)
    link_v[me] = mine

    pl.semaphore_wait(barrier, n)

    def link_copy(k, src):
        return pltpu.make_async_remote_copy(
            src_ref=link_v.at[src], dst_ref=link_v.at[src],
            send_sem=link_send.at[k], recv_sem=link_recv.at[src],
            device_id=(lax.rem(me + k, n), hd), device_id_type=MESH,
        )

    each(1, n, lambda k: link_copy(k, me).start())

    for i in range(3):
        loads[i].wait()
    kv_mine = jnp.dot(tok[...], kvw[...], preferred_element_type=F32).astype(BF16)
    kv[pl.ds(pl.multiple_of(me * t, t), t), :] = kv_mine

    def kv_block(src):
        return kv.at[pl.ds(pl.multiple_of(src * t, t), t), :]

    def kv_copy(src, target, send):
        return pltpu.make_async_remote_copy(
            src_ref=kv_block(src), dst_ref=kv_block(src),
            send_sem=send, recv_sem=kv_recv.at[src],
            device_id=(target, hd), device_id_type=MESH,
        )

    def row_copy(src, target, send):
        return pltpu.make_async_remote_copy(
            src_ref=rows.at[src], dst_ref=rows.at[src],
            send_sem=send, recv_sem=row_recv.at[src],
            device_id=(target, hd), device_id_type=MESH,
        )

    kv_set = (kv_copy, kv_send_a, kv_send_b, kv_send_c)
    row_set = (row_copy, row_send_a, row_send_b, row_send_c)

    def across(copy_of, send_a, send_b, send_c, k):
        return copy_of(me, ident(lax.rem(a + k, size), b, c), send_a.at[k])

    def to_b(copy_of, send_a, send_b, send_c, a_):
        return copy_of(ident(a_, b, c), ident(a, 1 - b, c), send_b.at[a_])

    def to_c(copy_of, send_a, send_b, send_c, a_, b_):
        return copy_of(ident(a_, b_, c), ident(a, b, 1 - c), send_c.at[a_ * 2 + b_])

    def first(group):
        each(1, size, lambda k: across(*group, k).start())
        to_b(*group, a).start()
        to_c(*group, a, b).start()

    def got(group, src):
        group[0](src, me, group[1].at[0]).wait_recv()

    def relay_a(group):
        def one(k):
            a_ = lax.rem(a + k, size)
            got(group, ident(a_, b, c))
            to_b(*group, a_).start()
            to_c(*group, a_, b).start()

        each(1, size, one)

    def relay_b(group):
        def one(k):
            a_ = lax.rem(a + k, size)
            got(group, ident(a_, 1 - b, c))
            to_c(*group, a_, 1 - b).start()

        each(0, size, one)

    def finish(group):
        def one(k):
            got(group, ident(k // 2, k % 2, 1 - c))

        each(0, 2 * size, one)

    def sent(group):
        each(1, size, lambda k: across(*group, k).wait_send())
        each(0, size, lambda k: to_b(*group, k).wait_send())
        each(0, 2 * size, lambda k: to_c(*group, k // 2, k % 2).wait_send())

    first(kv_set)

    each(1, n, lambda k: link_copy(k, lax.rem(me + k, n)).wait_recv())
    to_scalar = pltpu.make_async_copy(link_v, link_s, load_sem.at[6])
    to_scalar.start()
    to_scalar.wait()
    loads[3].wait()

    def link_at(s):
        return link_s[s // link_dev, 0, s % link_dev]

    def pick(s, carry):
        count, valid, chosen = carry
        v = link_at(s)
        safe = jnp.maximum(v, 0)
        own = jnp.where((v >= 0) & (lax.div(safe, entities) == me), 1, 0)
        local = lax.rem(safe, entities)
        chosen = tuple(
            jnp.where((own == 1) & (count == j), local, chosen[j]) for j in range(MOST)
        )
        return (count + own, valid + jnp.where(v >= 0, 1, 0), chosen)

    carry = (jnp.int32(0), jnp.int32(0), (jnp.int32(0),) * MOST)
    if slots <= 16:
        for s in range(slots):
            carry = pick(s, carry)
    else:
        carry = lax.fori_loop(0, slots, pick, carry)
    unused, valid_count, chosen = carry
    half = MOST * SUM_ROWS
    raw = jnp.concatenate([summ[chosen[j]] for j in range(MOST)], axis=0)
    r_out = lax.broadcasted_iota(jnp.int32, (2 * half, 2 * half), 0)
    r_in = lax.broadcasted_iota(jnp.int32, (2 * half, 2 * half), 1)
    perm = jnp.where(
        r_in == jnp.where(r_out < half, 2 * r_out, 2 * (r_out - half) + 1), 1.0, 0.0
    ).astype(BF16)
    split = jnp.dot(perm, raw, preferred_element_type=F32).astype(BF16)
    for j in range(2 * MOST):
        rows[me, j] = split[j * SUM_ROWS:(j + 1) * SUM_ROWS]
    first(row_set)

    loads[4].wait()

    def project(p):
        result = jnp.dot(
            tok[...], qw[:, p * 256:(p + 1) * 256], preferred_element_type=F32
        ).astype(BF16)
        for i in range(2):
            q[(2 * p + i) * t:(2 * p + i + 1) * t, :] = result[:, i * 128:(i + 1) * 128]

    pairs = heads // 2
    project(0)
    project(1)
    relay_a(kv_set)
    for p in range(2, pairs):
        project(p)
    relay_b(kv_set)
    relay_a(row_set)
    relay_b(row_set)
    finish(kv_set)
    finish(row_set)

    def place(s):
        v = link_at(s)
        safe = jnp.maximum(v, 0)
        owner = lax.div(safe, entities)

        def same(s2, total):
            w = link_at(s2)
            return total + jnp.where((w >= 0) & (lax.div(jnp.maximum(w, 0), entities) == owner), 1, 0)

        rank = jnp.int32(0)
        if slots <= 16:
            for s2 in range(s):
                rank = same(s2, rank)
        else:
            rank = lax.fori_loop(0, s, same, rank)
        rank = jnp.where(v >= 0, jnp.minimum(rank, MOST - 1), 0)
        start = n * t + s * SUM_ROWS
        if not isinstance(s, int):
            start = pl.multiple_of(start, SUM_ROWS)
        kv[pl.ds(start, SUM_ROWS), pl.ds(0, HEAD_DIM)] = rows[owner, rank]
        kv[pl.ds(start, SUM_ROWS), pl.ds(HEAD_DIM, HEAD_DIM)] = rows[owner, MOST + rank]

    if slots <= 16:
        for s in range(slots):
            place(s)
    else:
        lax.fori_loop(0, slots, lambda s, carry: (place(s), carry)[1], 0)

    factor = math.log2(math.e) / math.sqrt(HEAD_DIM)
    total_keys = kv.shape[0]
    chunk = 16 * t + 256
    if total_keys % chunk:
        chunk = t
    limit = n * t + valid_count * SUM_ROWS

    def attend(p, unused_carry):
        queries = q[pl.ds(pl.multiple_of(p * 2 * t, 2 * t), 2 * t), :]

        def one_chunk(i, state):
            top, total, accum = state
            start = i * chunk
            if not isinstance(i, int):
                start = pl.multiple_of(start, chunk)
            scores = lax.dot_general(
                queries, kv[pl.ds(start, chunk), pl.ds(0, HEAD_DIM)],
                (((1,), (1,)), ((), ())), preferred_element_type=F32,
            )
            column = lax.broadcasted_iota(jnp.int32, (1, chunk), 1) + start
            scores = jnp.where(column < limit, scores, -1e30)
            new_top = jnp.maximum(top, jnp.max(scores, axis=1, keepdims=True))
            change = jnp.exp2((top - new_top) * factor)
            weights = jnp.exp2((scores - new_top) * factor)
            total = total * change + jnp.sum(weights, axis=1, keepdims=True)
            product = jnp.dot(
                weights.astype(BF16), kv[pl.ds(start, chunk), pl.ds(HEAD_DIM, HEAD_DIM)],
                preferred_element_type=F32,
            )
            return (new_top, total, accum * change + product)

        state = (
            jnp.full((2 * t, 1), -1e30, F32),
            jnp.zeros((2 * t, 1), F32),
            jnp.zeros((2 * t, HEAD_DIM), F32),
        )
        if total_keys == chunk:
            state = one_chunk(0, state)
        else:
            state = lax.fori_loop(0, total_keys // chunk, one_chunk, state)
        result = (state[2] / state[1]).astype(BF16)
        att[2 * p] = result[:t]
        att[2 * p + 1] = result[t:]
        return unused_carry

    lax.fori_loop(0, pairs, attend, 0)

    loads[5].wait()
    attended = jnp.concatenate([att[h] for h in range(heads)], axis=1)
    width = out_ref.shape[1]
    pieces = y_send.shape[0]
    piece = width // pieces

    def y_copy(i):
        return pltpu.make_async_remote_copy(
            src_ref=y_send.at[i], dst_ref=y_recv.at[i],
            send_sem=y_send_sem.at[i], recv_sem=y_recv_sem.at[i],
            device_id=(me, 1 - hd), device_id_type=MESH,
        )

    def out_piece(side, i):
        start = pl.multiple_of(side * width + i * piece, piece)
        return jnp.dot(attended, ow[:, pl.ds(start, piece)], preferred_element_type=F32)

    for i in range(pieces):
        y_send[i] = out_piece(1 - hd, i).astype(BF16)
        y_copy(i).start()
    for i in range(pieces):
        part[:, i * piece:(i + 1) * piece] = out_piece(hd, i)
    for i in range(pieces):
        y_copy(i).wait_recv()
        out_ref[:, i * piece:(i + 1) * piece] = (
            part[:, i * piece:(i + 1) * piece] + y_recv[i].astype(F32)
        ).astype(BF16)
    for i in range(pieces):
        y_copy(i).wait_send()
    each(1, n, lambda k: link_copy(k, me).wait_send())
    sent(kv_set)
    sent(row_set)


def shards(n, tokens, q_weight, k_weight, v_weight, out_weight, summary, links):
    t, d = tokens.shape
    local = q_weight.shape[1]
    heads = local // HEAD_DIM
    width = out_weight.shape[1] // 2
    entities = summary.shape[0]
    link_dev = links.shape[0]
    pieces = 4
    size = n // 4
    flat = summary.reshape(entities, SUM_ROWS * 2, HEAD_DIM)
    dma = pltpu.SemaphoreType.DMA
    hbm = pl.BlockSpec(memory_space=pl.ANY)
    return pl.pallas_call(
        functools.partial(kernel, n, entities, link_dev),
        out_shape=jax.ShapeDtypeStruct((t, width), BF16),
        in_specs=[hbm] * 6 + [pl.BlockSpec(memory_space=pltpu.SMEM)],
        out_specs=pl.BlockSpec(memory_space=pltpu.VMEM),
        scratch_shapes=[
            pltpu.VMEM((t, d), BF16),
            pltpu.VMEM((d, local), BF16),
            pltpu.VMEM((d, 2 * HEAD_DIM), BF16),
            pltpu.VMEM(out_weight.shape, BF16),
            pltpu.VMEM(flat.shape, BF16),
            pltpu.VMEM((heads * t, HEAD_DIM), BF16),
            pltpu.VMEM((n * t + n * link_dev * SUM_ROWS, 2 * HEAD_DIM), BF16),
            pltpu.VMEM((n, 2 * MOST, SUM_ROWS, HEAD_DIM), BF16),
            pltpu.VMEM((n, 1, 128), jnp.int32),
            pltpu.SMEM((n, 1, 128), jnp.int32),
            pltpu.VMEM((heads, t, HEAD_DIM), BF16),
            pltpu.VMEM((t, width), F32),
            pltpu.VMEM((pieces, t, width // pieces), BF16),
            pltpu.VMEM((pieces, t, width // pieces), BF16),
            dma((7,)), dma((n,)), dma((n,)), dma((n,)), dma((n,)),
            dma((size,)), dma((size,)), dma((2 * size,)),
            dma((size,)), dma((size,)), dma((2 * size,)),
            dma((pieces,)), dma((pieces,)),
        ],
        compiler_params=pltpu.CompilerParams(
            collective_id=0, has_side_effects=True, vmem_limit_bytes=56 * 1024 * 1024
        ),
    )(tokens, q_weight, k_weight, v_weight, out_weight, flat, links)


def solution(mesh):
    placed = (
        P("seq", None),
        P(None, "head"),
        P(None, "head"),
        P(None, "head"),
        P("head", None),
        P("seq", None, None, "head"),
        P("seq"),
    )
    return jax.shard_map(
        functools.partial(shards, mesh.shape["seq"]),
        mesh=mesh, in_specs=placed, out_specs=P("seq", "head"), check_vma=False,
    )
```

```python
import functools
import math

import jax
import jax.numpy as jnp
from jax import lax
from jax.experimental import pallas as pl
from jax.experimental.pallas import tpu as pltpu
from jax.sharding import PartitionSpec as P

HEAD_DIM = 128
SUM_ROWS = 16
MOST = 3
MESH = pl.DeviceIdType.MESH
F32 = jnp.float32
BF16 = jnp.bfloat16


def each(low, high, step):
    if high - low <= 8:
        for i in range(low, high):
            step(i)
    else:
        lax.fori_loop(low, high, lambda i, carry: (step(i), carry)[1], 0)


def kernel(
    n, entities, link_dev,
    tok_hbm, qw_hbm, kw_hbm, vw_hbm, ow_hbm, sum_hbm, links_ref,
    out_ref,
    tok, qw, kvw, ow, summ, q, kv, rows, link_v, link_s, att, part, y_send, y_recv,
    top_ref, sum_ref, acc_ref,
    load_sem, kv_recv, row_recv, link_recv, link_send, link_recv_bc, link_send_bc,
    kv_send_a, kv_send_b, kv_send_c, row_send_a, row_send_b, row_send_c,
    y_send_sem, y_recv_sem,
):
    me = lax.axis_index("seq")
    hd = lax.axis_index("head")
    size = n // 4
    a, b, c = me // 4, (me // 2) % 2, me % 2
    slots = n * link_dev
    t = tok.shape[0]
    ht = t // 2
    heads = q.shape[0] // t
    block = heads * ht // 2
    part_keys = size * t

    def ident(a_, b_, c_):
        return (a_ * 2 + b_) * 2 + c_

    def place_of(a_, b_, c_):
        return (c_ * 2 + b_) * size + a_

    mine_at = place_of(a, b, c)

    def other(k):
        if size != 4:
            return lax.rem(a + k, size)
        end = 1 - ((a + 1) // 2) % 2
        if k == 1:
            return a + 1 - 2 * (a % 2)
        two, three = lax.rem(a + 2, 4), 3 - a
        return two * end + three * (1 - end) if k == 2 else three * end + two * (1 - end)

    loads = [
        pltpu.make_async_copy(tok_hbm, tok, load_sem.at[0]),
        pltpu.make_async_copy(kw_hbm, kvw.at[:, pl.ds(0, HEAD_DIM)], load_sem.at[1]),
        pltpu.make_async_copy(vw_hbm, kvw.at[:, pl.ds(HEAD_DIM, HEAD_DIM)], load_sem.at[2]),
        pltpu.make_async_copy(sum_hbm, summ, load_sem.at[3]),
        pltpu.make_async_copy(qw_hbm, qw, load_sem.at[4]),
        pltpu.make_async_copy(ow_hbm, ow, load_sem.at[5]),
    ]

    barrier = pltpu.get_barrier_semaphore()

    def greet(target, head):
        pl.semaphore_signal(barrier, inc=1, device_id=(target, head), device_id_type=MESH)

    each(1, size, lambda k: greet(ident(lax.rem(a + k, size), b, c), hd))
    greet(ident(a, 1 - b, c), hd)
    greet(ident(a, b, 1 - c), hd)
    greet(me, 1 - hd)
    for item in loads:
        item.start()

    lane = lax.broadcasted_iota(jnp.int32, (1, 128), 1)
    mine = jnp.full((1, 128), -1, jnp.int32)
    for i in range(link_dev):
        mine = jnp.where(lane == i, links_ref[i], mine)
    link_v[mine_at] = mine
    top_ref[...] = jnp.full(top_ref.shape, -1e30, F32)
    sum_ref[...] = jnp.zeros(sum_ref.shape, F32)
    acc_ref[...] = jnp.zeros(acc_ref.shape, F32)

    pl.semaphore_wait(barrier, size + 2)

    def link_a(src_a, target_a):
        at = place_of(src_a, b, c)
        return pltpu.make_async_remote_copy(
            src_ref=link_v.at[at], dst_ref=link_v.at[at],
            send_sem=link_send.at[target_a], recv_sem=link_recv.at[src_a],
            device_id=(ident(target_a, b, c), hd), device_id_type=MESH,
        )

    def link_b(b_, target_b):
        part_of = link_v.at[pl.ds((c * 2 + b_) * size, size)]
        return pltpu.make_async_remote_copy(
            src_ref=part_of, dst_ref=part_of,
            send_sem=link_send_bc.at[0], recv_sem=link_recv_bc.at[0],
            device_id=(ident(a, target_b, c), hd), device_id_type=MESH,
        )

    def link_c(c_, target_c):
        part_of = link_v.at[pl.ds(c_ * 2 * size, 2 * size)]
        return pltpu.make_async_remote_copy(
            src_ref=part_of, dst_ref=part_of,
            send_sem=link_send_bc.at[1], recv_sem=link_recv_bc.at[1],
            device_id=(ident(a, b, target_c), hd), device_id_type=MESH,
        )

    each(1, size, lambda k: link_a(a, lax.rem(a + k, size)).start())

    for i in range(3):
        loads[i].wait()
    kv_mine = jnp.dot(tok[...], kvw[...], preferred_element_type=F32).astype(BF16)
    kv[pl.ds(pl.multiple_of(mine_at * t, t), t), :] = kv_mine

    def kv_copy(src, target, send):
        held = kv.at[pl.ds(pl.multiple_of(src * t, t), t), :]
        return pltpu.make_async_remote_copy(
            src_ref=held, dst_ref=held,
            send_sem=send, recv_sem=kv_recv.at[src],
            device_id=(target, hd), device_id_type=MESH,
        )

    def row_copy(src, target, send):
        return pltpu.make_async_remote_copy(
            src_ref=rows.at[src], dst_ref=rows.at[src],
            send_sem=send, recv_sem=row_recv.at[src],
            device_id=(target, hd), device_id_type=MESH,
        )

    kv_set = (kv_copy, kv_send_a, kv_send_b, kv_send_c)
    row_set = (row_copy, row_send_a, row_send_b, row_send_c)

    def across(copy_of, send_a, send_b, send_c, k):
        a_ = other(k)
        return copy_of(mine_at, ident(a_, b, c), send_a.at[a_])

    def to_b(copy_of, send_a, send_b, send_c, a_):
        return copy_of(place_of(a_, b, c), ident(a, 1 - b, c), send_b.at[a_])

    def to_c(copy_of, send_a, send_b, send_c, a_, b_):
        return copy_of(place_of(a_, b_, c), ident(a, b, 1 - c), send_c.at[a_ * 2 + b_])

    def first(group):
        each(1, size, lambda k: across(*group, k).start())
        to_b(*group, a).start()
        to_c(*group, a, b).start()

    def got(group, src):
        group[0](src, me, group[1].at[0]).wait_recv()

    def relay_a(group):
        def one(k):
            a_ = other(k)
            got(group, place_of(a_, b, c))
            to_b(*group, a_).start()
            to_c(*group, a_, b).start()

        each(1, size, one)

    def relay_b(group):
        def one(k):
            a_ = a if isinstance(k, int) and k == 0 else other(k)
            got(group, place_of(a_, 1 - b, c))
            to_c(*group, a_, 1 - b).start()

        each(0, size, one)

    def finish(group, b_):
        each(0, size, lambda a_: got(group, place_of(a_, b_, 1 - c)))

    def sent(group):
        each(1, size, lambda k: across(*group, k).wait_send())
        each(0, size, lambda k: to_b(*group, k).wait_send())
        each(0, 2 * size, lambda k: to_c(*group, k // 2, k % 2).wait_send())

    first(kv_set)

    def project(p):
        result = jnp.dot(
            tok[...], qw[:, p * 256:(p + 1) * 256], preferred_element_type=F32
        ).astype(BF16)
        for i in range(2):
            for side in range(2):
                start = (side * heads + 2 * p + i) * ht
                q[start:start + ht, :] = result[side * ht:(side + 1) * ht, i * 128:(i + 1) * 128]

    pairs = heads // 2
    each(1, size, lambda k: link_a(lax.rem(a + k, size), a).wait_recv())
    link_b(b, 1 - b).start()
    loads[4].wait()
    project(0)
    link_b(1 - b, b).wait_recv()
    link_c(c, 1 - c).start()
    project(1)
    link_c(1 - c, c).wait_recv()
    to_scalar = pltpu.make_async_copy(link_v, link_s, load_sem.at[6])
    to_scalar.start()
    to_scalar.wait()
    loads[3].wait()

    def link_at(s):
        seat = s // link_dev
        return link_s[place_of(seat // 4, (seat // 2) % 2, seat % 2), 0, s % link_dev]

    def pick(s, carry):
        count, valid, chosen = carry
        v = link_at(s)
        safe = jnp.maximum(v, 0)
        own = jnp.where((v >= 0) & (lax.div(safe, entities) == me), 1, 0)
        local = lax.rem(safe, entities)
        chosen = tuple(
            jnp.where((own == 1) & (count == j), local, chosen[j]) for j in range(MOST)
        )
        return (count + own, valid + jnp.where(v >= 0, 1, 0), chosen)

    carry = (jnp.int32(0), jnp.int32(0), (jnp.int32(0),) * MOST)
    if slots <= 16:
        for s in range(slots):
            carry = pick(s, carry)
    else:
        carry = lax.fori_loop(0, slots, pick, carry)
    unused, valid_count, chosen = carry
    half = MOST * SUM_ROWS
    raw = jnp.concatenate([summ[chosen[j]] for j in range(MOST)], axis=0)
    r_out = lax.broadcasted_iota(jnp.int32, (2 * half, 2 * half), 0)
    r_in = lax.broadcasted_iota(jnp.int32, (2 * half, 2 * half), 1)
    perm = jnp.where(
        r_in == jnp.where(r_out < half, 2 * r_out, 2 * (r_out - half) + 1), 1.0, 0.0
    ).astype(BF16)
    split = jnp.dot(perm, raw, preferred_element_type=F32).astype(BF16)
    for j in range(2 * MOST):
        rows[mine_at, j] = split[j * SUM_ROWS:(j + 1) * SUM_ROWS]
    first(row_set)

    factor = math.log2(math.e) / math.sqrt(HEAD_DIM)
    limit = n * t + valid_count * SUM_ROWS

    def one_step(r0, start, count, masked):
        here = pl.ds(r0, block)
        scores = lax.dot_general(
            q[here, :], kv[pl.ds(start, count), pl.ds(0, HEAD_DIM)],
            (((1,), (1,)), ((), ())), preferred_element_type=F32,
        )
        if masked:
            column = lax.broadcasted_iota(jnp.int32, (1, count), 1) + start
            scores = jnp.where(column < limit, scores, -1e30)
        groups = [scores[:, g * 128:(g + 1) * 128] for g in range(count // 128)]
        old = top_ref[here, :]
        high = functools.reduce(jnp.maximum, groups)
        new = jnp.maximum(old, jnp.max(high, axis=1, keepdims=True))
        change = jnp.exp2((old - new) * factor)
        weights = [jnp.exp2((g - new) * factor) for g in groups]
        top_ref[here, :] = new
        sum_ref[here, :] = sum_ref[here, :] * change + functools.reduce(jnp.add, weights)
        product = jnp.dot(
            jnp.concatenate([w.astype(BF16) for w in weights], axis=1),
            kv[pl.ds(start, count), pl.ds(HEAD_DIM, HEAD_DIM)],
            preferred_element_type=F32,
        )
        acc_ref[here, :] = acc_ref[here, :] * change + product

    def attend(r0, start, count, masked=False):
        chunk = 512
        if count <= chunk or count % chunk:
            one_step(r0, start, count, masked)
        else:
            def body(i, carry):
                one_step(r0, pl.multiple_of(start + i * chunk, chunk // 2), chunk, masked)
                return carry

            lax.fori_loop(0, count // chunk, body, 0)

    def class_start(b_, c_):
        return pl.multiple_of((c_ * 2 + b_) * part_keys, part_keys)

    for p in range(2, pairs):
        project(p)
    relay_a(kv_set)
    relay_a(row_set)
    for r in range(4):
        attend(r * block, class_start(b, c), part_keys)
    relay_b(kv_set)
    finish(kv_set, b)
    for r in range(4):
        attend(r * block, class_start(b, 1 - c), part_keys)
    relay_b(row_set)
    for r in range(4):
        attend(r * block, class_start(1 - b, c), part_keys)
    finish(row_set, b)
    finish(row_set, 1 - b)

    def place(s):
        v = link_at(s)
        safe = jnp.maximum(v, 0)
        owner = lax.div(safe, entities)

        def same(s2, total):
            w = link_at(s2)
            return total + jnp.where((w >= 0) & (lax.div(jnp.maximum(w, 0), entities) == owner), 1, 0)

        rank = jnp.int32(0)
        if slots <= 16:
            for s2 in range(s):
                rank = same(s2, rank)
        else:
            rank = lax.fori_loop(0, s, same, rank)
        rank = jnp.where(v >= 0, jnp.minimum(rank, MOST - 1), 0)
        seat = place_of(
            lax.div(owner, 4), lax.rem(lax.div(owner, 2), 2), lax.rem(owner, 2)
        )
        start = n * t + s * SUM_ROWS
        if not isinstance(s, int):
            start = pl.multiple_of(start, SUM_ROWS)
        kv[pl.ds(start, SUM_ROWS), pl.ds(0, HEAD_DIM)] = rows[seat, rank]
        kv[pl.ds(start, SUM_ROWS), pl.ds(HEAD_DIM, HEAD_DIM)] = rows[seat, MOST + rank]

    if slots <= 16:
        for s in range(slots):
            place(s)
    else:
        lax.fori_loop(0, slots, lambda s, carry: (place(s), carry)[1], 0)
    finish(kv_set, 1 - b)
    loads[5].wait()

    width = out_ref.shape[1]
    per_side = y_send.shape[0] // 2
    piece = width // per_side

    def y_copy(i):
        return pltpu.make_async_remote_copy(
            src_ref=y_send.at[i], dst_ref=y_recv.at[i],
            send_sem=y_send_sem.at[i], recv_sem=y_recv_sem.at[i],
            device_id=(me, 1 - hd), device_id_type=MESH,
        )

    for side in range(2):
        for r in range(2):
            r0 = (side * 2 + r) * block
            attend(r0, class_start(1 - b, 1 - c), part_keys)
            attend(r0, n * t, slots * SUM_ROWS, True)
            total = jnp.sum(sum_ref[pl.ds(r0, block), :], axis=1, keepdims=True)
            result = (acc_ref[pl.ds(r0, block), :] / total).astype(BF16)
            for i in range(heads // 2):
                h = r * (heads // 2) + i
                att[side, :, h * 128:(h + 1) * 128] = result[i * ht:(i + 1) * ht]
        for i in range(per_side):
            start = pl.multiple_of((1 - hd) * width + i * piece, piece)
            y_send[side * per_side + i] = jnp.dot(
                att[side], ow[:, pl.ds(start, piece)], preferred_element_type=F32
            ).astype(BF16)
            y_copy(side * per_side + i).start()
    both = jnp.concatenate([att[0], att[1]], axis=0)
    for i in range(per_side):
        start = pl.multiple_of(hd * width + i * piece, piece)
        part[:, i * piece:(i + 1) * piece] = jnp.dot(
            both, ow[:, pl.ds(start, piece)], preferred_element_type=F32
        )
    each(1, size, lambda k: link_a(a, lax.rem(a + k, size)).wait_send())
    link_b(b, 1 - b).wait_send()
    link_c(c, 1 - c).wait_send()
    sent(kv_set)
    sent(row_set)
    for side in range(2):
        for i in range(per_side):
            y_copy(side * per_side + i).wait_recv()
            here = (slice(side * ht, (side + 1) * ht), slice(i * piece, (i + 1) * piece))
            out_ref[here] = (part[here] + y_recv[side * per_side + i].astype(F32)).astype(BF16)
    for i in range(2 * per_side):
        y_copy(i).wait_send()


def shards(n, tokens, q_weight, k_weight, v_weight, out_weight, summary, links):
    t, d = tokens.shape
    local = q_weight.shape[1]
    heads = local // HEAD_DIM
    width = out_weight.shape[1] // 2
    entities = summary.shape[0]
    link_dev = links.shape[0]
    pieces = 2
    size = n // 4
    flat = summary.reshape(entities, SUM_ROWS * 2, HEAD_DIM)
    dma = pltpu.SemaphoreType.DMA
    hbm = pl.BlockSpec(memory_space=pl.ANY)
    return pl.pallas_call(
        functools.partial(kernel, n, entities, link_dev),
        out_shape=jax.ShapeDtypeStruct((t, width), BF16),
        in_specs=[hbm] * 6 + [pl.BlockSpec(memory_space=pltpu.SMEM)],
        out_specs=pl.BlockSpec(memory_space=pltpu.VMEM),
        scratch_shapes=[
            pltpu.VMEM((t, d), BF16),
            pltpu.VMEM((d, local), BF16),
            pltpu.VMEM((d, 2 * HEAD_DIM), BF16),
            pltpu.VMEM(out_weight.shape, BF16),
            pltpu.VMEM(flat.shape, BF16),
            pltpu.VMEM((heads * t, HEAD_DIM), BF16),
            pltpu.VMEM((n * t + n * link_dev * SUM_ROWS, 2 * HEAD_DIM), BF16),
            pltpu.VMEM((n, 2 * MOST, SUM_ROWS, HEAD_DIM), BF16),
            pltpu.VMEM((n, 1, 128), jnp.int32),
            pltpu.SMEM((n, 1, 128), jnp.int32),
            pltpu.VMEM((2, t // 2, local), BF16),
            pltpu.VMEM((t, width), F32),
            pltpu.VMEM((2 * pieces, t // 2, width // pieces), BF16),
            pltpu.VMEM((2 * pieces, t // 2, width // pieces), BF16),
            pltpu.VMEM((heads * t, HEAD_DIM), F32),
            pltpu.VMEM((heads * t, HEAD_DIM), F32),
            pltpu.VMEM((heads * t, HEAD_DIM), F32),
            dma((7,)), dma((n,)), dma((n,)), dma((size,)), dma((size,)), dma((2,)), dma((2,)),
            dma((size,)), dma((size,)), dma((2 * size,)),
            dma((size,)), dma((size,)), dma((2 * size,)),
            dma((2 * pieces,)), dma((2 * pieces,)),
        ],
        compiler_params=pltpu.CompilerParams(
            collective_id=0, has_side_effects=True, vmem_limit_bytes=56 * 1024 * 1024
        ),
    )(tokens, q_weight, k_weight, v_weight, out_weight, flat, links)


def solution(mesh):
    placed = (
        P("seq", None),
        P(None, "head"),
        P(None, "head"),
        P(None, "head"),
        P("head", None),
        P("seq", None, None, "head"),
        P("seq"),
    )
    return jax.shard_map(
        functools.partial(shards, mesh.shape["seq"]),
        mesh=mesh, in_specs=placed, out_specs=P("seq", "head"), check_vma=False,
    )
```

```python
import functools
import math

import jax
import jax.numpy as jnp
from jax import lax
from jax.experimental import pallas as pl
from jax.experimental.pallas import tpu as pltpu
from jax.sharding import PartitionSpec as P

HEAD_DIM = 128
SUM_ROWS = 16
MOST = 3
MESH = pl.DeviceIdType.MESH
F32 = jnp.float32
BF16 = jnp.bfloat16


def each(low, high, step):
    if high - low <= 8:
        for i in range(low, high):
            step(i)
    else:
        lax.fori_loop(low, high, lambda i, carry: (step(i), carry)[1], 0)


def kernel(
    n, entities, link_dev,
    tok_hbm, qw_hbm, kw_hbm, vw_hbm, ow_hbm, sum_hbm, links_ref,
    out_ref,
    tok, qw, kvw, ow, summ, q, kv, rows, link_v, link_s, att, part, y_send, y_recv,
    top_ref, sum_ref, acc_ref,
    load_sem, kv_recv, row_recv, link_recv, link_send, link_recv_bc, link_send_bc,
    kv_send_a, kv_send_b, kv_send_c, row_send_a, row_send_b, row_send_c,
    y_send_sem, y_recv_sem,
):
    me = lax.axis_index("seq")
    hd = lax.axis_index("head")
    size = n // 4
    a, b, c = me // 4, (me // 2) % 2, me % 2
    slots = n * link_dev
    t = tok.shape[0]
    ht = t // 2
    heads = q.shape[0] // t
    block = heads * ht // 2
    part_keys = size * t

    def ident(a_, b_, c_):
        return (a_ * 2 + b_) * 2 + c_

    def place_of(a_, b_, c_):
        return (c_ * 2 + b_) * size + a_

    mine_at = place_of(a, b, c)

    def other(k):
        if size != 4:
            return lax.rem(a + k, size)
        end = 1 - ((a + 1) // 2) % 2
        if k == 1:
            return a + 1 - 2 * (a % 2)
        two, three = lax.rem(a + 2, 4), 3 - a
        return two * end + three * (1 - end) if k == 2 else three * end + two * (1 - end)

    loads = [
        pltpu.make_async_copy(tok_hbm, tok, load_sem.at[0]),
        pltpu.make_async_copy(kw_hbm, kvw.at[:, pl.ds(0, HEAD_DIM)], load_sem.at[1]),
        pltpu.make_async_copy(vw_hbm, kvw.at[:, pl.ds(HEAD_DIM, HEAD_DIM)], load_sem.at[2]),
        pltpu.make_async_copy(sum_hbm, summ, load_sem.at[3]),
        pltpu.make_async_copy(qw_hbm, qw, load_sem.at[4]),
        pltpu.make_async_copy(ow_hbm, ow, load_sem.at[5]),
    ]

    barrier = pltpu.get_barrier_semaphore()

    def greet(target, head):
        pl.semaphore_signal(barrier, inc=1, device_id=(target, head), device_id_type=MESH)

    each(1, size, lambda k: greet(ident(lax.rem(a + k, size), b, c), hd))
    greet(ident(a, 1 - b, c), hd)
    greet(ident(a, b, 1 - c), hd)
    greet(ident(a, 1 - b, 1 - c), hd)
    greet(me, 1 - hd)
    for item in loads:
        item.start()

    lane = lax.broadcasted_iota(jnp.int32, (1, 128), 1)
    mine = jnp.full((1, 128), -1, jnp.int32)
    for i in range(link_dev):
        mine = jnp.where(lane == i, links_ref[i], mine)
    link_v[mine_at] = mine
    top_ref[...] = jnp.full(top_ref.shape, -1e30, F32)
    sum_ref[...] = jnp.zeros(sum_ref.shape, F32)
    acc_ref[...] = jnp.zeros(acc_ref.shape, F32)

    pl.semaphore_wait(barrier, size + 3)

    def link_a(src_a, target_a):
        at = place_of(src_a, b, c)
        return pltpu.make_async_remote_copy(
            src_ref=link_v.at[at], dst_ref=link_v.at[at],
            send_sem=link_send.at[target_a], recv_sem=link_recv.at[src_a],
            device_id=(ident(target_a, b, c), hd), device_id_type=MESH,
        )

    def link_bc(src_b, src_c, target_b, target_c, k):
        part_of = link_v.at[pl.ds((src_c * 2 + src_b) * size, size)]
        return pltpu.make_async_remote_copy(
            src_ref=part_of, dst_ref=part_of,
            send_sem=link_send_bc.at[k], recv_sem=link_recv_bc.at[k],
            device_id=(ident(a, target_b, target_c), hd), device_id_type=MESH,
        )

    corners = ((1 - b, 1 - c), (1 - b, c), (b, 1 - c))

    each(1, size, lambda k: link_a(a, lax.rem(a + k, size)).start())

    for i in range(3):
        loads[i].wait()
    kv_mine = jnp.dot(tok[...], kvw[...], preferred_element_type=F32).astype(BF16)
    kv[pl.ds(pl.multiple_of(mine_at * t, t), t), :] = kv_mine

    def kv_copy(src, target, send):
        held = kv.at[pl.ds(pl.multiple_of(src * t, t), t), :]
        return pltpu.make_async_remote_copy(
            src_ref=held, dst_ref=held,
            send_sem=send, recv_sem=kv_recv.at[src],
            device_id=(target, hd), device_id_type=MESH,
        )

    def row_copy(src, target, send):
        return pltpu.make_async_remote_copy(
            src_ref=rows.at[src], dst_ref=rows.at[src],
            send_sem=send, recv_sem=row_recv.at[src],
            device_id=(target, hd), device_id_type=MESH,
        )

    kv_set = (kv_copy, kv_send_a, kv_send_b, kv_send_c)
    row_set = (row_copy, row_send_a, row_send_b, row_send_c)

    def across(copy_of, send_a, send_b, send_c, k):
        a_ = other(k)
        return copy_of(mine_at, ident(a_, b, c), send_a.at[a_])

    def to_b(copy_of, send_a, send_b, send_c, a_):
        return copy_of(place_of(a_, b, c), ident(a, 1 - b, c), send_b.at[a_])

    def to_c(copy_of, send_a, send_b, send_c, a_, b_):
        return copy_of(place_of(a_, b_, c), ident(a, b, 1 - c), send_c.at[a_ * 2 + b_])

    def first(group):
        each(1, size, lambda k: across(*group, k).start())
        to_b(*group, a).start()
        to_c(*group, a, b).start()

    def got(group, src):
        group[0](src, me, group[1].at[0]).wait_recv()

    def relay_a(group, low, high):
        def one(k):
            a_ = other(k)
            got(group, place_of(a_, b, c))
            to_b(*group, a_).start()
            to_c(*group, a_, b).start()

        each(low, high, one)

    def relay_b(group):
        def one(k):
            a_ = a if isinstance(k, int) and k == 0 else other(k)
            got(group, place_of(a_, 1 - b, c))
            to_c(*group, a_, 1 - b).start()

        each(0, size, one)

    def finish(group, b_):
        each(0, size, lambda a_: got(group, place_of(a_, b_, 1 - c)))

    def sent(group):
        each(1, size, lambda k: across(*group, k).wait_send())
        each(0, size, lambda k: to_b(*group, k).wait_send())
        each(0, 2 * size, lambda k: to_c(*group, k // 2, k % 2).wait_send())

    first(kv_set)

    def project(p):
        result = jnp.dot(
            tok[...], qw[:, p * 256:(p + 1) * 256], preferred_element_type=F32
        ).astype(BF16)
        for i in range(2):
            for side in range(2):
                start = (side * heads + 2 * p + i) * ht
                q[start:start + ht, :] = result[side * ht:(side + 1) * ht, i * 128:(i + 1) * 128]

    pairs = heads // 2
    each(1, size, lambda k: link_a(lax.rem(a + k, size), a).wait_recv())
    for k in range(3):
        link_bc(b, c, *corners[k], k).start()
    loads[4].wait()
    project(0)
    project(1)
    relay_a(kv_set, 1, 2)
    for k in range(3):
        link_bc(*corners[k], b, c, k).wait_recv()
    to_scalar = pltpu.make_async_copy(link_v, link_s, load_sem.at[6])
    to_scalar.start()
    to_scalar.wait()
    loads[3].wait()

    def link_at(s):
        seat = s // link_dev
        return link_s[place_of(seat // 4, (seat // 2) % 2, seat % 2), 0, s % link_dev]

    def pick(s, carry):
        count, valid, chosen = carry
        v = link_at(s)
        safe = jnp.maximum(v, 0)
        own = jnp.where((v >= 0) & (lax.div(safe, entities) == me), 1, 0)
        local = lax.rem(safe, entities)
        chosen = tuple(
            jnp.where((own == 1) & (count == j), local, chosen[j]) for j in range(MOST)
        )
        return (count + own, valid + jnp.where(v >= 0, 1, 0), chosen)

    carry = (jnp.int32(0), jnp.int32(0), (jnp.int32(0),) * MOST)
    if slots <= 16:
        for s in range(slots):
            carry = pick(s, carry)
    else:
        carry = lax.fori_loop(0, slots, pick, carry)
    unused, valid_count, chosen = carry
    half = MOST * SUM_ROWS
    raw = jnp.concatenate([summ[chosen[j]] for j in range(MOST)], axis=0)
    r_out = lax.broadcasted_iota(jnp.int32, (2 * half, 2 * half), 0)
    r_in = lax.broadcasted_iota(jnp.int32, (2 * half, 2 * half), 1)
    perm = jnp.where(
        r_in == jnp.where(r_out < half, 2 * r_out, 2 * (r_out - half) + 1), 1.0, 0.0
    ).astype(BF16)
    split = jnp.dot(perm, raw, preferred_element_type=F32).astype(BF16)
    for j in range(2 * MOST):
        rows[mine_at, j] = split[j * SUM_ROWS:(j + 1) * SUM_ROWS]
    first(row_set)

    factor = math.log2(math.e) / math.sqrt(HEAD_DIM)
    limit = n * t + valid_count * SUM_ROWS

    def one_step(r0, start, count, masked):
        here = pl.ds(r0, block)
        scores = lax.dot_general(
            q[here, :], kv[pl.ds(start, count), pl.ds(0, HEAD_DIM)],
            (((1,), (1,)), ((), ())), preferred_element_type=F32,
        )
        if masked:
            column = lax.broadcasted_iota(jnp.int32, (1, count), 1) + start
            scores = jnp.where(column < limit, scores, -1e30)
        groups = [scores[:, g * 128:(g + 1) * 128] for g in range(count // 128)]
        old = top_ref[here, :]
        high = functools.reduce(jnp.maximum, groups)
        new = jnp.maximum(old, jnp.max(high, axis=1, keepdims=True))
        change = jnp.exp2((old - new) * factor)
        weights = [jnp.exp2((g - new) * factor) for g in groups]
        top_ref[here, :] = new
        sum_ref[here, :] = sum_ref[here, :] * change + functools.reduce(jnp.add, weights)
        product = jnp.dot(
            jnp.concatenate([w.astype(BF16) for w in weights], axis=1),
            kv[pl.ds(start, count), pl.ds(HEAD_DIM, HEAD_DIM)],
            preferred_element_type=F32,
        )
        acc_ref[here, :] = acc_ref[here, :] * change + product

    def attend(r0, start, count, masked=False):
        chunk = 512
        if count <= chunk or count % chunk:
            one_step(r0, start, count, masked)
        else:
            def body(i, carry):
                one_step(r0, pl.multiple_of(start + i * chunk, chunk // 2), chunk, masked)
                return carry

            lax.fori_loop(0, count // chunk, body, 0)

    def class_start(b_, c_):
        return pl.multiple_of((c_ * 2 + b_) * part_keys, part_keys)

    relay_a(kv_set, 2, size)
    for p in range(2, pairs):
        project(p)
    for r in range(4):
        attend(r * block, class_start(b, c), part_keys)
    relay_b(kv_set)
    relay_a(row_set, 1, size)
    finish(kv_set, b)
    for r in range(4):
        attend(r * block, class_start(b, 1 - c), part_keys)
    relay_b(row_set)
    for r in range(4):
        attend(r * block, class_start(1 - b, c), part_keys)
    finish(kv_set, 1 - b)
    for r in range(4):
        attend(r * block, class_start(1 - b, 1 - c), part_keys)
    finish(row_set, b)
    finish(row_set, 1 - b)

    def place(s):
        v = link_at(s)
        safe = jnp.maximum(v, 0)
        owner = lax.div(safe, entities)

        def same(s2, total):
            w = link_at(s2)
            return total + jnp.where((w >= 0) & (lax.div(jnp.maximum(w, 0), entities) == owner), 1, 0)

        rank = jnp.int32(0)
        if slots <= 16:
            for s2 in range(s):
                rank = same(s2, rank)
        else:
            rank = lax.fori_loop(0, s, same, rank)
        rank = jnp.where(v >= 0, jnp.minimum(rank, MOST - 1), 0)
        seat = place_of(
            lax.div(owner, 4), lax.rem(lax.div(owner, 2), 2), lax.rem(owner, 2)
        )
        start = n * t + s * SUM_ROWS
        if not isinstance(s, int):
            start = pl.multiple_of(start, SUM_ROWS)
        kv[pl.ds(start, SUM_ROWS), pl.ds(0, HEAD_DIM)] = rows[seat, rank]
        kv[pl.ds(start, SUM_ROWS), pl.ds(HEAD_DIM, HEAD_DIM)] = rows[seat, MOST + rank]

    if slots <= 16:
        for s in range(slots):
            place(s)
    else:
        lax.fori_loop(0, slots, lambda s, carry: (place(s), carry)[1], 0)
    loads[5].wait()

    width = out_ref.shape[1]
    per_side = y_send.shape[0] // 2
    piece = width // per_side

    def y_copy(i):
        return pltpu.make_async_remote_copy(
            src_ref=y_send.at[i], dst_ref=y_recv.at[i],
            send_sem=y_send_sem.at[i], recv_sem=y_recv_sem.at[i],
            device_id=(me, 1 - hd), device_id_type=MESH,
        )

    for side in range(2):
        for r in range(2):
            r0 = (side * 2 + r) * block
            attend(r0, n * t, slots * SUM_ROWS, True)
            total = jnp.sum(sum_ref[pl.ds(r0, block), :], axis=1, keepdims=True)
            result = (acc_ref[pl.ds(r0, block), :] / total).astype(BF16)
            for i in range(heads // 2):
                h = r * (heads // 2) + i
                att[side, :, h * 128:(h + 1) * 128] = result[i * ht:(i + 1) * ht]
        for i in range(per_side):
            start = pl.multiple_of((1 - hd) * width + i * piece, piece)
            y_send[side * per_side + i] = jnp.dot(
                att[side], ow[:, pl.ds(start, piece)], preferred_element_type=F32
            ).astype(BF16)
            y_copy(side * per_side + i).start()
    both = jnp.concatenate([att[0], att[1]], axis=0)
    for i in range(per_side):
        start = pl.multiple_of(hd * width + i * piece, piece)
        part[:, i * piece:(i + 1) * piece] = jnp.dot(
            both, ow[:, pl.ds(start, piece)], preferred_element_type=F32
        )
    each(1, size, lambda k: link_a(a, lax.rem(a + k, size)).wait_send())
    for k in range(3):
        link_bc(b, c, *corners[k], k).wait_send()
    sent(kv_set)
    sent(row_set)
    for side in range(2):
        for i in range(per_side):
            y_copy(side * per_side + i).wait_recv()
            here = (slice(side * ht, (side + 1) * ht), slice(i * piece, (i + 1) * piece))
            out_ref[here] = (part[here] + y_recv[side * per_side + i].astype(F32)).astype(BF16)
    for i in range(2 * per_side):
        y_copy(i).wait_send()


def shards(n, tokens, q_weight, k_weight, v_weight, out_weight, summary, links):
    t, d = tokens.shape
    local = q_weight.shape[1]
    heads = local // HEAD_DIM
    width = out_weight.shape[1] // 2
    entities = summary.shape[0]
    link_dev = links.shape[0]
    pieces = 2
    size = n // 4
    flat = summary.reshape(entities, SUM_ROWS * 2, HEAD_DIM)
    dma = pltpu.SemaphoreType.DMA
    hbm = pl.BlockSpec(memory_space=pl.ANY)
    return pl.pallas_call(
        functools.partial(kernel, n, entities, link_dev),
        out_shape=jax.ShapeDtypeStruct((t, width), BF16),
        in_specs=[hbm] * 6 + [pl.BlockSpec(memory_space=pltpu.SMEM)],
        out_specs=pl.BlockSpec(memory_space=pltpu.VMEM),
        scratch_shapes=[
            pltpu.VMEM((t, d), BF16),
            pltpu.VMEM((d, local), BF16),
            pltpu.VMEM((d, 2 * HEAD_DIM), BF16),
            pltpu.VMEM(out_weight.shape, BF16),
            pltpu.VMEM(flat.shape, BF16),
            pltpu.VMEM((heads * t, HEAD_DIM), BF16),
            pltpu.VMEM((n * t + n * link_dev * SUM_ROWS, 2 * HEAD_DIM), BF16),
            pltpu.VMEM((n, 2 * MOST, SUM_ROWS, HEAD_DIM), BF16),
            pltpu.VMEM((n, 1, 128), jnp.int32),
            pltpu.SMEM((n, 1, 128), jnp.int32),
            pltpu.VMEM((2, t // 2, local), BF16),
            pltpu.VMEM((t, width), F32),
            pltpu.VMEM((2 * pieces, t // 2, width // pieces), BF16),
            pltpu.VMEM((2 * pieces, t // 2, width // pieces), BF16),
            pltpu.VMEM((heads * t, HEAD_DIM), F32),
            pltpu.VMEM((heads * t, HEAD_DIM), F32),
            pltpu.VMEM((heads * t, HEAD_DIM), F32),
            dma((7,)), dma((n,)), dma((n,)), dma((size,)), dma((size,)), dma((3,)), dma((3,)),
            dma((size,)), dma((size,)), dma((2 * size,)),
            dma((size,)), dma((size,)), dma((2 * size,)),
            dma((2 * pieces,)), dma((2 * pieces,)),
        ],
        compiler_params=pltpu.CompilerParams(
            collective_id=0, has_side_effects=True, vmem_limit_bytes=56 * 1024 * 1024
        ),
    )(tokens, q_weight, k_weight, v_weight, out_weight, flat, links)


def solution(mesh):
    placed = (
        P("seq", None),
        P(None, "head"),
        P(None, "head"),
        P(None, "head"),
        P("head", None),
        P("seq", None, None, "head"),
        P("seq"),
    )
    return jax.shard_map(
        functools.partial(shards, mesh.shape["seq"]),
        mesh=mesh, in_specs=placed, out_specs=P("seq", "head"), check_vma=False,
    )
```
